32 devices in a mesh: ctx: 4 (over z), lag: 4 (over x, core), chan: 2 (over y).
Axes of the slice: x: 2, y: 2, z: 4, core: 2. Of those that a mesh axis runs over, the one named last changes fastest.
Arguments:
- values: bfloat16 [512, 8192], P('ctx', 'chan'), may hold values from -6 to 6
- gate: bfloat16 [512, 8192], P('ctx', ('chan', 'lag')), may hold values from -6 to 6
- bias: float32 [8192], P('chan'), may hold values from -6 to 6
- filter_taps: bfloat16 [512, 8192], P('ctx', 'chan'), may hold values from -2 to 2
Outputs:
- mixed: bfloat16 [512, 8192], P('ctx', ('chan', 'lag'))
The draws below stay inside these ranges and needn't reach their ends.
All inputs are finite; a program needn't handle non-finite values.
Results may differ from the reference program's by a relative error of at most 0.006.
Values may be sent and summed in bfloat16 or wider, within the bound.
No kernel may reach another device: no remote copies, remote signals or barrier semaphores. Data moves between devices by JAX's collectives and lax.ppermute only.
A program may use at most 64 MiB of HBM per device.

```python
import math
import jax
import jax.numpy as jnp

CHANNELS = 8192
STREAM_ITEMS = 512


def draw_filter_taps(key, part):
    stochastic_seeds = jax.random.split(jax.random.fold_in(key, 7), 6)
    item_step_index = jnp.arange(STREAM_ITEMS, dtype=jnp.float32)[:, None]
    share_slow = 0.5
    slow = jax.random.uniform(stochastic_seeds[0], (1, CHANNELS)) < share_slow
    slow_rate = jnp.exp(jax.random.uniform(stochastic_seeds[1], (1, CHANNELS), minval=math.log(0.05), maxval=math.log(0.6))) / STREAM_ITEMS
    fast_rate = jnp.exp(jax.random.uniform(stochastic_seeds[2], (1, CHANNELS), minval=math.log(1.0 / 50.0), maxval=math.log(1.0 / 30.0)))
    rates = jnp.where(slow, slow_rate, fast_rate)
    spike_onset_step = jax.random.randint(stochastic_seeds[3], (2,), 1, STREAM_ITEMS).astype(jnp.float32)
    falloff_factors = jax.random.uniform(stochastic_seeds[4], (2, CHANNELS), minval=0.2, maxval=0.5)
    logarithmic_amplitude_profile = -rates * item_step_index
    logarithmic_amplitude_profile = logarithmic_amplitude_profile + jnp.where(item_step_index >= spike_onset_step[0], jnp.log(1.0 - falloff_factors[0])[None, :], 0.0)
    logarithmic_amplitude_profile = logarithmic_amplitude_profile + jnp.where(item_step_index >= spike_onset_step[1], jnp.log(1.0 - falloff_factors[1])[None, :], 0.0)
    envelope = jnp.exp(logarithmic_amplitude_profile)
    noise = jnp.clip(jax.random.normal(stochastic_seeds[5], (STREAM_ITEMS, CHANNELS), jnp.float32), -5.0, 5.0)
    scale = 1.0 / jnp.sqrt(jnp.sum(envelope * envelope, axis=0, keepdims=True))
    return jnp.clip(noise * envelope * scale, -2.0, 2.0).astype(jnp.bfloat16)


def shard_levels(key, dims, cuts, smallest, high):
    factor_of, own = 1.0, jax.random.fold_in(key, 6)
    for dim, parts in cuts:
        steps = jnp.exp(jax.random.uniform(jax.random.fold_in(own, dim), (parts,), jnp.float32, smallest / len(cuts), high / len(cuts)))
        factor_of = factor_of * jnp.repeat(steps, dims[dim] // parts).reshape([-1 if axis == dim else 1 for axis in range(len(dims))])
    return factor_of


def gaussian(key, shape, width, limit, shards=(), kind=jnp.bfloat16):
    drawn = width * jax.random.normal(key, shape, jnp.float32)
    if shards:
        drawn = drawn * shard_levels(key, shape, shards, -0.22, 0.18)
    return jnp.clip(drawn, -limit, limit).astype(kind)


def setup_inputs(seed: int = 0) -> dict:
    key_list = jax.random.split(jax.random.key(seed), 5)
    return {
        "values": gaussian(key_list[0], (STREAM_ITEMS, CHANNELS), 1.0, 6.0, ((0, 4), (1, 2))),
        "gate": gaussian(key_list[1], (STREAM_ITEMS, CHANNELS), 1.0, 6.0, ((0, 4), (1, 8))),
        "bias": gaussian(key_list[2], (CHANNELS,), 1.0, 6.0, ((0, 2),), jnp.float32),
        "filter_taps": draw_filter_taps(jax.random.fold_in(key_list[4], 71), 0),
    }


def reference(values, gate, bias, filter_taps):
    value_data = values.astype(jnp.float32)
    taps_data = filter_taps.astype(jnp.float32)
    padded_length = 2 * STREAM_ITEMS
    value_freq = jnp.fft.rfft(value_data, n=padded_length, axis=0)
    taps_freq = jnp.fft.rfft(taps_data, n=padded_length, axis=0)
    convolved = jnp.fft.irfft(value_freq * taps_freq, n=padded_length, axis=0)[:STREAM_ITEMS]
    convolved = convolved.astype(jnp.float32)
    mixed = gate.astype(jnp.float32) * (convolved + bias[None, :] * value_data)
    return mixed.astype(jnp.bfloat16)
```

```python
import functools

import jax
import jax.numpy as jnp
import ml_dtypes
import numpy as np
from jax import lax
from jax.experimental import pallas as pl
from jax.experimental.pallas import tpu as pltpu
from jax.sharding import PartitionSpec as P

LANES = 128
MIB = 1 << 20


def split(table):
    upper = table.astype(ml_dtypes.bfloat16)
    lower = (table - upper.astype(np.float64)).astype(ml_dtypes.bfloat16)
    return upper, lower


def dft_tables(rows):
    length = 2 * rows
    frequency = np.concatenate([np.arange(0, rows, 2), np.arange(1, rows, 2)])
    odd = 2 * frequency[:, None] + 1
    angle = 2.0 * np.pi * (odd * np.arange(rows)[None, :] % (2 * length)) / (2 * length)
    forward = np.concatenate([np.cos(angle), -np.sin(angle)], 0)
    back = np.concatenate([np.cos(angle.T), -np.sin(angle.T)], 1) / rows
    upper, lower = split(back)
    return np.concatenate(split(forward), 1), np.concatenate([upper, lower, upper], 1)


def to(count, me, step):
    return lax.rem(me + step, count)


def came(count, me, step):
    return lax.rem(me - step + count, count)


def ring(count, step):
    return [(i, (i + step) % count) for i in range(count)]


def dot(a, b):
    return jnp.dot(a, b, preferred_element_type=jnp.float32)


def take(values, taps, count, chunks, lanes):
    me = lax.axis_index("ctx")
    first = lax.axis_index("lag") * (count * chunks * lanes)

    def piece(chunk, step):
        start = first + (to(count, me, step) * chunks + chunk) * lanes
        return jnp.concatenate(
            [lax.dynamic_slice_in_dim(array, start, lanes, 1) for array in (values, taps)], 1
        )

    return [[piece(chunk, step) for step in range(count)] for chunk in range(chunks)]


def conv_kernel(count, *refs):
    pieces = refs[:count]
    bias, forward, back = refs[count : count + 3]
    outs = refs[count + 3 : 2 * count + 3]
    blocks, spectrum, total, result = refs[2 * count + 3 :]
    rows, lanes = outs[0].shape
    me = lax.axis_index("ctx")
    table = forward[...]
    for step in range(count):
        i = came(count, me, step)
        x = pieces[step][...]
        blocks[i] = x[:, :lanes]
        spectrum[i] = dot(table, jnp.concatenate([x, x], 0))

    def tile(t, sign):
        re = pl.ds(pl.multiple_of(t * 8, 8), 8)
        im = pl.ds(pl.multiple_of(rows + t * 8, 8), 8)
        val_re = [spectrum[i, re, :lanes] for i in range(count)]
        val_im = [spectrum[i, im, :lanes] for i in range(count)]
        tap_re = [spectrum[i, re, lanes:] for i in range(count)]
        tap_im = [spectrum[i, im, lanes:] for i in range(count)]
        last_re = last_im = 0.0
        for r in range(count):
            sum_re = sum_im = 0.0
            for i in range(r + 1):
                a, b, c, d = val_re[i], val_im[i], tap_re[r - i], tap_im[r - i]
                sum_re = sum_re + (a * c - b * d)
                sum_im = sum_im + (a * d + b * c)
            total[r, re, :] = sum_re - sign * last_im
            total[r, im, :] = sum_im + sign * last_re
            last_re, last_im = sum_re, sum_im

    half = rows // 16
    pl.loop(0, half)(lambda t: tile(t, 1.0))
    pl.loop(half, 2 * half)(lambda t: tile(t, -1.0))

    for r in range(count):
        y = total[r]
        upper = y.astype(jnp.bfloat16)
        lower = (y - upper.astype(jnp.float32)).astype(jnp.bfloat16)
        conv = dot(back[...], jnp.concatenate([upper, upper, lower], 0))
        skip = bias[...] * blocks[r].astype(jnp.float32)
        result[r] = (conv + skip).astype(jnp.bfloat16)
    for step in range(count):
        outs[step][...] = result[to(count, me, step)]


def convolve(arrived, bias, forward, back):
    count = len(arrived)
    rows, lanes = arrived[0].shape[0], arrived[0].shape[1] // 2
    vmem = pl.BlockSpec(memory_space=pltpu.VMEM)
    return pl.pallas_call(
        functools.partial(conv_kernel, count),
        out_shape=[jax.ShapeDtypeStruct((rows, lanes), jnp.bfloat16)] * count,
        in_specs=[vmem] * (count + 3),
        out_specs=[vmem] * count,
        scratch_shapes=[
            pltpu.VMEM((count, rows, lanes), jnp.bfloat16),
            pltpu.VMEM((count, 2 * rows, 2 * lanes), jnp.float32),
            pltpu.VMEM((count, 2 * rows, lanes), jnp.float32),
            pltpu.VMEM((count, rows, lanes), jnp.bfloat16),
        ],
        compiler_params=pltpu.CompilerParams(vmem_limit_bytes=16 * MIB),
        name="convolve",
    )(*arrived, bias, forward, back)


def gate_kernel(count, chunks, lanes, *refs):
    pieces, gate, out = refs[:-2], refs[-2], refs[-1]
    me = lax.axis_index("ctx")
    for step in range(count):
        owner = came(count, me, step)
        for chunk in range(chunks):
            cols = pl.ds(pl.multiple_of((owner * chunks + chunk) * lanes, LANES), lanes)
            mixed = gate[:, cols].astype(jnp.float32) * pieces[chunk * count + step][...].astype(
                jnp.float32
            )
            out[:, cols] = mixed.astype(jnp.bfloat16)


def apply_gate(returned, gate):
    chunks, count = len(returned), len(returned[0])
    lanes = returned[0][0].shape[1]
    pieces = [piece for group in returned for piece in group]
    if lanes % LANES == 0:
        vmem = pl.BlockSpec(memory_space=pltpu.VMEM)
        return pl.pallas_call(
            functools.partial(gate_kernel, count, chunks, lanes),
            out_shape=jax.ShapeDtypeStruct(gate.shape, jnp.bfloat16),
            in_specs=[vmem] * (len(pieces) + 1),
            out_specs=vmem,
            compiler_params=pltpu.CompilerParams(vmem_limit_bytes=2 * MIB),
            name="gate",
        )(*pieces, gate)
    me = lax.axis_index("ctx")
    stacked = jnp.stack(pieces).reshape(chunks, count, gate.shape[0], lanes)
    ordered = jnp.roll(stacked[:, ::-1], me + 1, 1)
    whole = jnp.transpose(ordered, (2, 1, 0, 3)).reshape(gate.shape)
    return (gate.astype(jnp.float32) * whole.astype(jnp.float32)).astype(jnp.bfloat16)


def exchange(pieces):
    count = len(pieces)
    return [pieces[0]] + [
        lax.ppermute(pieces[step], "ctx", ring(count, step))
        for step in range(1, count)
    ]


def body(values, gate, bias, filter_taps):
    rows, share = gate.shape
    count = lax.axis_size("ctx")
    narrow = share // count
    lanes = narrow if narrow % LANES else LANES * 2
    chunks = narrow // lanes
    forward, back = (jnp.asarray(table) for table in dft_tables(rows))
    first = (lax.axis_index("lag") * count + lax.axis_index("ctx")) * narrow
    own_bias = lax.dynamic_slice_in_dim(bias, first, narrow, 0).reshape(chunks, 1, lanes)
    pieces = take(values, filter_taps, count, chunks, lanes)
    arrived = [exchange(group) for group in pieces]
    returned = [
        exchange(convolve(group, own_bias[chunk], forward, back))
        for chunk, group in enumerate(arrived)
    ]
    return apply_gate(returned, gate)


def solution(mesh):
    return jax.shard_map(
        body,
        mesh=mesh,
        in_specs=(P("ctx", "chan"), P("ctx", ("chan", "lag")), P("chan"), P("ctx", "chan")),
        out_specs=P("ctx", ("chan", "lag")),
        check_vma=False,
    )
```

```python
import functools

import jax
import jax.numpy as jnp
import ml_dtypes
import numpy as np
from jax import lax
from jax.experimental import pallas as pl
from jax.experimental.pallas import tpu as pltpu
from jax.sharding import PartitionSpec as P

LANES = 128
MIB = 1 << 20
VMEM = pl.BlockSpec(memory_space=pltpu.VMEM)
OUT = ("swap", 2, 1, 3)
BACK = ("ring", 1, 2, 3)


def split(table):
    upper = table.astype(ml_dtypes.bfloat16)
    lower = (table - upper.astype(np.float64)).astype(ml_dtypes.bfloat16)
    return upper, lower


def dft_tables(rows):
    length = 2 * rows
    frequency = np.concatenate([np.arange(0, rows, 2), np.arange(1, rows, 2)])
    odd = 2 * frequency[:, None] + 1
    angle = 2.0 * np.pi * (odd * np.arange(rows)[None, :] % (2 * length)) / (2 * length)
    forward = np.concatenate([np.cos(angle), -np.sin(angle)], 0)
    back = np.concatenate([np.cos(angle.T), -np.sin(angle.T)], 1) / rows
    upper, lower = split(back)
    return np.concatenate(split(forward), 1), np.concatenate([upper, lower, upper], 1)


def steps(plan, count):
    return list(plan[1:]) if count == 4 else list(range(1, count))


def swaps(plan, count):
    return plan[0] == "swap" and count & (count - 1) == 0


def to(plan, count, me, step):
    return me ^ step if swaps(plan, count) else lax.rem(me + step, count)


def came(plan, count, me, step):
    return me ^ step if swaps(plan, count) else lax.rem(me - step + count, count)


def pairs(plan, count, step):
    if swaps(plan, count):
        return [(i, i ^ step) for i in range(count)]
    return [(i, (i + step) % count) for i in range(count)]


def dot(a, b):
    return jnp.dot(a, b, preferred_element_type=jnp.float32)


def take(values, taps, count, lanes):
    me = lax.axis_index("ctx")
    first = lax.axis_index("lag") * (count * lanes)
    later = lax.optimization_barrier((values, taps))

    def piece(step, arrays):
        start = first + to(OUT, count, me, step) * lanes
        return jnp.concatenate(
            [lax.dynamic_slice_in_dim(array, start, lanes, 1) for array in arrays], 1
        )

    order = steps(OUT, count)
    pieces = {step: piece(step, (values, taps) if step == order[0] else later) for step in order}
    return piece(0, later), [pieces[step] for step in order]


def transform_into(plan, step, piece, table, spectra):
    count = spectra.shape[0]
    x = piece[...]
    owner = came(plan, count, lax.axis_index("ctx"), step)
    spectra[owner] = dot(table[...], jnp.concatenate([x, x], 0))


def transform_kernel(step, *refs):
    piece, table, spectra = refs[0], refs[1], refs[-1]
    transform_into(OUT, step, piece, table, spectra)


def transform(spectra, step, piece, table, count):
    shape = jax.ShapeDtypeStruct((count, table.shape[0], piece.shape[1]), jnp.float32)
    held = [] if spectra is None else [spectra]
    return pl.pallas_call(
        functools.partial(transform_kernel, step),
        out_shape=shape,
        in_specs=[VMEM] * (2 + len(held)),
        out_specs=VMEM,
        input_output_aliases={2: 0} if held else {},
        compiler_params=pltpu.CompilerParams(vmem_limit_bytes=2 * MIB),
        cost_estimate=pl.CostEstimate(
            flops=2 * table.size * piece.shape[1],
            bytes_accessed=8 * piece.size,
            transcendentals=0,
        ),
        name="transform",
    )(piece, table, *held)


def conv_kernel(count, step, piece, bias, forward, back, _, spectra, *refs):
    outs, total, result = refs[:count], refs[count], refs[count + 1]
    rows, lanes = outs[0].shape
    me = lax.axis_index("ctx")
    transform_into(OUT, step, piece, forward, spectra)
    width = min(lanes, LANES)
    base = 0
    if lanes % LANES == 0:
        base = pl.multiple_of((lax.axis_index("lag") * count + me) * lanes, LANES)

    def tile(t, sign):
        re = pl.ds(pl.multiple_of(t * 8, 8), 8)
        im = pl.ds(pl.multiple_of(rows + t * 8, 8), 8)
        for first in range(0, lanes, width):
            val = slice(first, first + width)
            tap = slice(lanes + first, lanes + first + width)
            val_re = [spectra[i, re, val] for i in range(count)]
            val_im = [spectra[i, im, val] for i in range(count)]
            tap_re = [spectra[i, re, tap] for i in range(count)]
            tap_im = [spectra[i, im, tap] for i in range(count)]
            tap_re[0] = tap_re[0] + bias[:, pl.ds(base + first, width)]
            last_re = last_im = 0.0
            for r in range(count):
                sum_re = sum_im = 0.0
                for i in range(r + 1):
                    a, b, c, d = val_re[i], val_im[i], tap_re[r - i], tap_im[r - i]
                    sum_re = sum_re + (a * c - b * d)
                    sum_im = sum_im + (a * d + b * c)
                total[r, re, val] = sum_re - sign * last_im
                total[r, im, val] = sum_im + sign * last_re
                last_re, last_im = sum_re, sum_im

    half = rows // 16
    unroll = half if count <= 4 else 1
    pl.loop(0, half, unroll=unroll)(lambda t: tile(t, 1.0))
    pl.loop(half, 2 * half, unroll=unroll)(lambda t: tile(t, -1.0))

    for r in range(count):
        y = total[r]
        upper = y.astype(jnp.bfloat16)
        lower = (y - upper.astype(jnp.float32)).astype(jnp.bfloat16)
        conv = dot(back[...], jnp.concatenate([upper, upper, lower], 0))
        result[r] = conv.astype(jnp.bfloat16)
    for place, step_back in enumerate([0] + steps(BACK, count)):
        outs[place][...] = result[to(BACK, count, me, step_back)]


def convolve(spectra, step, piece, bias, forward, back):
    count, length, both = spectra.shape
    rows, lanes = length // 2, both // 2
    outs = pl.pallas_call(
        functools.partial(conv_kernel, count, step),
        out_shape=[jax.ShapeDtypeStruct(spectra.shape, jnp.float32)]
        + [jax.ShapeDtypeStruct((rows, lanes), jnp.bfloat16)] * count,
        in_specs=[VMEM] * 5,
        out_specs=[VMEM] * (count + 1),
        scratch_shapes=[
            pltpu.VMEM((count, length, lanes), jnp.float32),
            pltpu.VMEM((count, rows, lanes), jnp.bfloat16),
        ],
        input_output_aliases={4: 0},
        compiler_params=pltpu.CompilerParams(vmem_limit_bytes=8 * MIB),
        name="convolve",
    )(piece, bias, forward, back, spectra)
    return outs[1:]


def gate_kernel(count, lanes, *refs):
    pieces, gate, out = refs[:count], refs[count], refs[count + 1]
    me = lax.axis_index("ctx")
    for place, step in enumerate([0] + steps(BACK, count)):
        cols = pl.ds(pl.multiple_of(came(BACK, count, me, step) * lanes, LANES), lanes)
        mixed = gate[:, cols].astype(jnp.float32) * pieces[place][...].astype(jnp.float32)
        out[:, cols] = mixed.astype(jnp.bfloat16)


def apply_gate(returned, gate):
    count = len(returned)
    lanes = returned[0].shape[1]
    if lanes % LANES == 0:
        return pl.pallas_call(
            functools.partial(gate_kernel, count, lanes),
            out_shape=jax.ShapeDtypeStruct(gate.shape, jnp.bfloat16),
            in_specs=[VMEM] * (count + 1),
            out_specs=VMEM,
            compiler_params=pltpu.CompilerParams(vmem_limit_bytes=2 * MIB),
            name="gate",
        )(*returned, gate)
    me = lax.axis_index("ctx")
    ordered = jnp.roll(jnp.stack(returned)[::-1], me + 1, 0)
    whole = jnp.transpose(ordered, (1, 0, 2)).reshape(gate.shape)
    return (gate.astype(jnp.float32) * whole.astype(jnp.float32)).astype(jnp.bfloat16)


def move(plan, count, step, piece):
    return lax.ppermute(piece, "ctx", pairs(plan, count, step))


def body(values, gate, bias, filter_taps):
    rows, share = gate.shape
    count = lax.axis_size("ctx")
    lanes = share // count
    forward, back = (jnp.asarray(table) for table in dft_tables(rows))
    own_bias = bias.reshape(1, -1)
    if lanes % LANES:
        start = (lax.axis_index("lag") * count + lax.axis_index("ctx")) * lanes
        own_bias = lax.dynamic_slice_in_dim(own_bias, start, lanes, 1)
    own, pieces = take(values, filter_taps, count, lanes)
    out_steps, back_steps = steps(OUT, count), steps(BACK, count)
    arrived = [move(OUT, count, step, piece) for step, piece in zip(out_steps, pieces)]
    spectra = transform(None, 0, own, forward, count)
    for step, piece in zip(out_steps[:-1], arrived):
        spectra = transform(spectra, step, piece, forward, count)
    done = convolve(spectra, out_steps[-1], arrived[-1], own_bias, forward, back)
    returned = [move(BACK, count, step, piece) for step, piece in zip(back_steps, done[1:])]
    return apply_gate([done[0]] + returned, gate)


def solution(mesh):
    return jax.shard_map(
        body,
        mesh=mesh,
        in_specs=(P("ctx", "chan"), P("ctx", ("chan", "lag")), P("chan"), P("ctx", "chan")),
        out_specs=P("ctx", ("chan", "lag")),
        check_vma=False,
    )
```

```python
import functools

import jax
import jax.numpy as jnp
import ml_dtypes
import numpy as np
from jax import lax
from jax.experimental import pallas as pl
from jax.experimental.pallas import tpu as pltpu
from jax.sharding import PartitionSpec as P

LANES = 128
MIB = 1 << 20
VMEM = pl.BlockSpec(memory_space=pltpu.VMEM)
OUT = ("swap", 3, 1, 2)
BACK = ("ring", 2, 1, 3)


def split(table):
    upper = table.astype(ml_dtypes.bfloat16)
    lower = (table - upper.astype(np.float64)).astype(ml_dtypes.bfloat16)
    return upper, lower


def dft_tables(rows):
    length = 2 * rows
    frequency = np.concatenate([np.arange(0, rows, 2), np.arange(1, rows, 2)])
    odd = 2 * frequency[:, None] + 1
    angle = 2.0 * np.pi * (odd * np.arange(rows)[None, :] % (2 * length)) / (2 * length)
    forward = np.concatenate([np.cos(angle), -np.sin(angle)], 0)
    back = np.concatenate([np.cos(angle.T), -np.sin(angle.T)], 1) / rows
    upper, lower = split(back)
    return np.concatenate(split(forward), 1), np.concatenate([upper, lower, upper], 1)


def steps(plan, count):
    return list(plan[1:]) if count == 4 else list(range(1, count))


def swaps(plan, count):
    return plan[0] == "swap" and count & (count - 1) == 0


def to(plan, count, me, step):
    return me ^ step if swaps(plan, count) else lax.rem(me + step, count)


def came(plan, count, me, step):
    return me ^ step if swaps(plan, count) else lax.rem(me - step + count, count)


def pairs(plan, count, step):
    if swaps(plan, count):
        return [(i, i ^ step) for i in range(count)]
    return [(i, (i + step) % count) for i in range(count)]


def dot(a, b):
    return jnp.dot(a, b, preferred_element_type=jnp.float32)


def take(values, taps, count, lanes):
    me = lax.axis_index("ctx")
    first = lax.axis_index("lag") * (count * lanes)
    later = lax.optimization_barrier((values, taps))

    def piece(step, arrays):
        start = first + to(OUT, count, me, step) * lanes
        return jnp.concatenate(
            [lax.dynamic_slice_in_dim(array, start, lanes, 1) for array in arrays], 1
        )

    order = steps(OUT, count)
    pieces = {step: piece(step, (values, taps) if step == order[0] else later) for step in order}
    return piece(0, later), [pieces[step] for step in order]


def transform_into(plan, step, piece, table, spectra):
    count = spectra.shape[0]
    x = piece[...]
    owner = came(plan, count, lax.axis_index("ctx"), step)
    spectra[owner] = dot(table[...], jnp.concatenate([x, x], 0))


def transform_kernel(step, *refs):
    piece, table, spectra = refs[0], refs[1], refs[-1]
    transform_into(OUT, step, piece, table, spectra)


def transform(spectra, step, piece, table, count, after=()):
    shape = jax.ShapeDtypeStruct((count, table.shape[0], piece.shape[1]), jnp.float32)
    held = [] if spectra is None else [spectra]
    return pl.pallas_call(
        functools.partial(transform_kernel, step),
        out_shape=shape,
        in_specs=[VMEM] * (2 + len(held) + len(after)),
        out_specs=VMEM,
        input_output_aliases={2: 0} if held else {},
        compiler_params=pltpu.CompilerParams(vmem_limit_bytes=2 * MIB),
        cost_estimate=pl.CostEstimate(
            flops=2 * table.size * piece.shape[1],
            bytes_accessed=8 * piece.size,
            transcendentals=0,
        ),
        name="transform",
    )(piece, table, *held, *after)


def bias_base(count, lanes):
    if lanes % LANES:
        return 0
    first = (lax.axis_index("lag") * count + lax.axis_index("ctx")) * lanes
    return pl.multiple_of(first, LANES)


def inverse(y, back):
    upper = y.astype(jnp.bfloat16)
    lower = (y - upper.astype(jnp.float32)).astype(jnp.bfloat16)
    return dot(back[...], jnp.concatenate([upper, upper, lower], 0)).astype(jnp.bfloat16)


def products(spectra, bias, sums, total, ready, wanted, closes):
    count, length, both = spectra.shape
    rows, lanes = length // 2, both // 2
    width = min(lanes, LANES)
    base = bias_base(count, lanes)
    meets = [[i for i in range(r + 1) if wanted(i, r - i)] for r in range(count)]
    values = sorted({i for r in range(count) for i in meets[r]})
    taps = sorted({r - i for r in range(count) for i in meets[r]})

    def tile(t, sign):
        re = pl.ds(pl.multiple_of(t * 8, 8), 8)
        im = pl.ds(pl.multiple_of(rows + t * 8, 8), 8)
        for first in range(0, lanes, width):
            val = slice(first, first + width)
            tap = slice(lanes + first, lanes + first + width)
            val_re = {i: spectra[i, re, val] for i in values}
            val_im = {i: spectra[i, im, val] for i in values}
            tap_re = {j: spectra[j, re, tap] for j in taps}
            tap_im = {j: spectra[j, im, tap] for j in taps}
            if 0 in taps:
                tap_re[0] = tap_re[0] + bias[:, pl.ds(base + first, width)]
            last_re = last_im = None
            for r in range(count):
                sum_re = sum_im = None
                if r in ready:
                    sum_re, sum_im = sums[r, re, val], sums[r, im, val]
                for i in meets[r]:
                    a, b, c, d = val_re[i], val_im[i], tap_re[r - i], tap_im[r - i]
                    new_re, new_im = a * c - b * d, a * d + b * c
                    sum_re = new_re if sum_re is None else sum_re + new_re
                    sum_im = new_im if sum_im is None else sum_im + new_im
                if closes(r):
                    total[r, re, val] = sum_re if r == 0 else sum_re - sign * last_im
                    total[r, im, val] = sum_im if r == 0 else sum_im + sign * last_re
                if sums is not None and meets[r] and r not in ready:
                    sums[r, re, val] = sum_re
                    sums[r, im, val] = sum_im
                last_re, last_im = sum_re, sum_im

    half = rows // 16
    unroll = half if count <= 4 else 1
    pl.loop(0, half, unroll=unroll)(lambda t: tile(t, 1.0))
    pl.loop(half, 2 * half, unroll=unroll)(lambda t: tile(t, -1.0))


def early_kernel(count, last, bias, back, spectra, sums, early, total):
    missing = came(OUT, count, lax.axis_index("ctx"), last)
    for m in range(count):

        @pl.when(missing == m)
        def _(m=m):
            products(
                spectra, bias, sums, total, (), lambda i, j: m not in (i, j), lambda r: r < m
            )
            for r in range(m):
                early[r] = inverse(total[r], back)


def late_kernel(count, last, piece, bias, forward, back, sums, early, _, spectra, *refs):
    outs, total, result = refs[:count], refs[count], refs[count + 1]
    me = lax.axis_index("ctx")
    missing = came(OUT, count, me, last)
    transform_into(OUT, last, piece, forward, spectra)
    for m in range(count):

        @pl.when(missing == m)
        def _(m=m):
            ready = [r for r in range(count) if any(m not in (i, r - i) for i in range(r + 1))]
            products(
                spectra, bias, sums, total, ready, lambda i, j: m in (i, j), lambda r: r >= m
            )
            for r in range(count):
                result[r] = early[r] if r < m else inverse(total[r], back)

    for place, step in enumerate([0] + steps(BACK, count)):
        outs[place][...] = result[to(BACK, count, me, step)]


def whole_kernel(count, last, piece, bias, forward, back, _, spectra, *refs):
    outs, total, result = refs[:count], refs[count], refs[count + 1]
    me = lax.axis_index("ctx")
    transform_into(OUT, last, piece, forward, spectra)
    products(spectra, bias, None, total, (), lambda i, j: True, lambda r: True)
    for r in range(count):
        result[r] = inverse(total[r], back)
    for place, step in enumerate([0] + steps(BACK, count)):
        outs[place][...] = result[to(BACK, count, me, step)]


def convolve(spectra, last, piece, bias, forward, back):
    count, length, both = spectra.shape
    rows, lanes = length // 2, both // 2
    totals = jax.ShapeDtypeStruct((count, length, lanes), jnp.float32)
    results = jax.ShapeDtypeStruct((count, rows, lanes), jnp.bfloat16)
    held = []
    if count <= 4:
        held = pl.pallas_call(
            functools.partial(early_kernel, count, last),
            out_shape=[totals, results],
            in_specs=[VMEM] * 3,
            out_specs=[VMEM] * 2,
            scratch_shapes=[pltpu.VMEM(totals.shape, totals.dtype)],
            compiler_params=pltpu.CompilerParams(vmem_limit_bytes=4 * MIB),
            cost_estimate=pl.CostEstimate(
                flops=3 * 2 * back.size * lanes, bytes_accessed=4 * spectra.size, transcendentals=0
            ),
            name="early_products",
        )(bias, back, spectra)
    return pl.pallas_call(
        functools.partial(late_kernel if held else whole_kernel, count, last),
        out_shape=[jax.ShapeDtypeStruct(spectra.shape, jnp.float32)]
        + [jax.ShapeDtypeStruct((rows, lanes), jnp.bfloat16)] * count,
        in_specs=[VMEM] * (5 + len(held)),
        out_specs=[VMEM] * (count + 1),
        scratch_shapes=[
            pltpu.VMEM(totals.shape, totals.dtype),
            pltpu.VMEM(results.shape, results.dtype),
        ],
        input_output_aliases={4 + len(held): 0},
        compiler_params=pltpu.CompilerParams(vmem_limit_bytes=8 * MIB),
        name="convolve",
    )(piece, bias, forward, back, *held, spectra)[1:]


def gated(gate, cols, piece):
    return (gate[:, cols].astype(jnp.float32) * piece.astype(jnp.float32)).astype(jnp.bfloat16)


def first_block_kernel(count, lanes, *refs):
    pieces = refs[: count - 1]
    bias, forward, back, gate, out, token, spectrum, total, mixed, sem = refs[count - 1 :]
    rows = out.shape[0]
    lag = lax.axis_index("lag")
    token[...] = jnp.zeros_like(token)

    @pl.when(lax.axis_index("ctx") == 0)
    def _():
        for step, piece in zip(steps(OUT, count), pieces):
            owner = step
            cols = slice(owner * lanes, (owner + 1) * lanes)
            x = piece[...]
            spectrum[...] = dot(forward[...], jnp.concatenate([x, x], 0))
            start = pl.multiple_of((lag * count + owner) * lanes, LANES)
            a, b = spectrum[:rows, :lanes], spectrum[rows:, :lanes]
            c = spectrum[:rows, lanes:] + bias[:, pl.ds(start, lanes)]
            d = spectrum[rows:, lanes:]
            total[:rows] = a * c - b * d
            total[rows:] = a * d + b * c
            mixed[:, cols] = gated(gate, cols, inverse(total[...], back))
        copy = pltpu.make_async_copy(mixed.at[:, lanes:], out.at[:, lanes:], sem)
        copy.start()
        copy.wait()


def first_block(pieces, bias, forward, back, gate):
    count = len(pieces) + 1
    lanes = pieces[0].shape[1] // 2
    length = forward.shape[0]
    return pl.pallas_call(
        functools.partial(first_block_kernel, count, lanes),
        out_shape=[
            jax.ShapeDtypeStruct(gate.shape, jnp.bfloat16),
            jax.ShapeDtypeStruct((8, LANES), jnp.float32),
        ],
        in_specs=[VMEM] * (count + 3),
        out_specs=[pl.BlockSpec(memory_space=pltpu.HBM), VMEM],
        scratch_shapes=[
            pltpu.VMEM((length, 2 * lanes), jnp.float32),
            pltpu.VMEM((length, lanes), jnp.float32),
            pltpu.VMEM(gate.shape, jnp.bfloat16),
            pltpu.SemaphoreType.DMA,
        ],
        compiler_params=pltpu.CompilerParams(vmem_limit_bytes=4 * MIB),
        cost_estimate=pl.CostEstimate(
            flops=2 * (count - 1) * forward.size * 2 * lanes, bytes_accessed=0, transcendentals=0
        ),
        name="first_block",
    )(*pieces, bias, forward, back, gate)


def put_kernel(places, count, *refs):
    pieces, gate, out, mixed, sems = refs[: len(places)], refs[-5], refs[-3], refs[-2], refs[-1]
    lanes = pieces[0].shape[1]
    me = lax.axis_index("ctx")
    order = [0] + steps(BACK, count)

    def put(todo):
        copies = []
        for k in todo:
            owner = came(BACK, count, me, order[places[k]])
            cols = pl.ds(pl.multiple_of(owner * lanes, LANES), lanes)
            mixed[k] = gated(gate, cols, pieces[k][...])
            copies.append(pltpu.make_async_copy(mixed.at[k], out.at[:, cols], sems.at[k]))
            copies[-1].start()
        for copy in copies:
            copy.wait()

    mine = [k for k, place in enumerate(places) if place == 0]
    if mine:
        put(mine)

    @pl.when(me != 0)
    def _():
        put([k for k in range(len(places)) if k not in mine])


def put(places, pieces, gate, out):
    count = gate.shape[1] // pieces[0].shape[1]
    hbm = pl.BlockSpec(memory_space=pltpu.HBM)
    return pl.pallas_call(
        functools.partial(put_kernel, places, count),
        out_shape=jax.ShapeDtypeStruct(gate.shape, jnp.bfloat16),
        in_specs=[VMEM] * (len(pieces) + 1) + [hbm],
        out_specs=hbm,
        scratch_shapes=[
            pltpu.VMEM((len(places),) + pieces[0].shape, jnp.bfloat16),
            pltpu.SemaphoreType.DMA((len(places),)),
        ],
        input_output_aliases={len(pieces) + 1: 0},
        compiler_params=pltpu.CompilerParams(vmem_limit_bytes=MIB),
        name="put",
    )(*pieces, gate, out)


def apply_gate(returned, gate):
    me = lax.axis_index("ctx")
    ordered = jnp.roll(jnp.stack(returned)[::-1], me + 1, 0)
    whole = jnp.transpose(ordered, (1, 0, 2)).reshape(gate.shape)
    return (gate.astype(jnp.float32) * whole.astype(jnp.float32)).astype(jnp.bfloat16)


def move(plan, count, step, piece):
    return lax.ppermute(piece, "ctx", pairs(plan, count, step))


def body(values, gate, bias, filter_taps):
    rows, share = gate.shape
    count = lax.axis_size("ctx")
    lanes = share // count
    forward, back = (jnp.asarray(table) for table in dft_tables(rows))
    own_bias = bias.reshape(1, -1)
    if lanes % LANES:
        start = (lax.axis_index("lag") * count + lax.axis_index("ctx")) * lanes
        own_bias = lax.dynamic_slice_in_dim(own_bias, start, lanes, 1)
    own, pieces = take(values, filter_taps, count, lanes)
    out_steps, back_steps = steps(OUT, count), steps(BACK, count)
    arrived = [move(OUT, count, step, piece) for step, piece in zip(out_steps, pieces)]
    spectra = transform(None, 0, own, forward, count)
    after = []
    if lanes % LANES == 0:
        out, *after = first_block(pieces, own_bias, forward, back, gate)
    for step, piece in zip(out_steps[:-1], arrived):
        spectra = transform(spectra, step, piece, forward, count, after)
        after = []
    done = convolve(spectra, out_steps[-1], arrived[-1], own_bias, forward, back)
    returned = [move(BACK, count, step, piece) for step, piece in zip(back_steps, done[1:])]
    if lanes % LANES:
        return apply_gate([done[0]] + returned, gate)
    out = put((0,), done[:1], gate, out)
    return put(tuple(range(1, count)), returned, gate, out)


def solution(mesh):
    return jax.shard_map(
        body,
        mesh=mesh,
        in_specs=(P("ctx", "chan"), P("ctx", ("chan", "lag")), P("chan"), P("ctx", "chan")),
        out_specs=P("ctx", ("chan", "lag")),
        check_vma=False,
    )
```

```python
import functools

import jax
import jax.numpy as jnp
import ml_dtypes
import numpy as np
from jax import lax
from jax.experimental import pallas as pl
from jax.experimental.pallas import tpu as pltpu
from jax.sharding import PartitionSpec as P

LANES = 128
MIB = 1 << 20
VMEM = pl.BlockSpec(memory_space=pltpu.VMEM)
OUT = ("swap", 3, 1, 2)
BACK = ("ring", 2, 1, 3)


def split(table):
    upper = table.astype(ml_dtypes.bfloat16)
    lower = (table - upper.astype(np.float64)).astype(ml_dtypes.bfloat16)
    return upper, lower


def dft_tables(rows):
    length = 2 * rows
    frequency = np.concatenate([np.arange(0, rows, 2), np.arange(1, rows, 2)])
    odd = 2 * frequency[:, None] + 1
    angle = 2.0 * np.pi * (odd * np.arange(rows)[None, :] % (2 * length)) / (2 * length)
    forward = np.concatenate([np.cos(angle), -np.sin(angle)], 0)
    back = np.concatenate([np.cos(angle.T), -np.sin(angle.T)], 1) / rows
    upper, lower = split(back)
    return np.concatenate(split(forward), 1), np.concatenate([upper, lower, upper], 1)


def steps(plan, count):
    return list(plan[1:]) if count == 4 else list(range(1, count))


def swaps(plan, count):
    return plan[0] == "swap" and count & (count - 1) == 0


def to(plan, count, me, step):
    return me ^ step if swaps(plan, count) else lax.rem(me + step, count)


def came(plan, count, me, step):
    return me ^ step if swaps(plan, count) else lax.rem(me - step + count, count)


def pairs(plan, count, step):
    if swaps(plan, count):
        return [(i, i ^ step) for i in range(count)]
    return [(i, (i + step) % count) for i in range(count)]


def dot(a, b):
    return jnp.dot(a, b, preferred_element_type=jnp.float32)


def take(values, taps, count, lanes):
    me = lax.axis_index("ctx")
    first = lax.axis_index("lag") * (count * lanes)
    later = lax.optimization_barrier((values, taps))

    def piece(step, arrays):
        start = first + to(OUT, count, me, step) * lanes
        return jnp.concatenate(
            [lax.dynamic_slice_in_dim(array, start, lanes, 1) for array in arrays], 1
        )

    order = steps(OUT, count)
    pieces = {step: piece(step, (values, taps) if step == order[0] else later) for step in order}
    return piece(0, later), [pieces[step] for step in order]


def transform_into(plan, step, piece, table, spectra):
    count = spectra.shape[0]
    x = piece[...]
    owner = came(plan, count, lax.axis_index("ctx"), step)
    spectra[owner] = dot(table[...], jnp.concatenate([x, x], 0))


def transform_kernel(step, *refs):
    piece, table, spectra = refs[0], refs[1], refs[-1]
    if step:
        spectra[...] = refs[2][...]
    transform_into(OUT, step, piece, table, spectra)


def transform(spectra, step, piece, table, count, after=()):
    shape = jax.ShapeDtypeStruct((count, table.shape[0], piece.shape[1]), jnp.float32)
    held = [] if spectra is None else [spectra]
    return pl.pallas_call(
        functools.partial(transform_kernel, step),
        out_shape=shape,
        in_specs=[VMEM] * (2 + len(held) + len(after)),
        out_specs=VMEM,
        input_output_aliases={2: 0} if held else {},
        compiler_params=pltpu.CompilerParams(vmem_limit_bytes=2 * MIB),
        cost_estimate=pl.CostEstimate(
            flops=2 * table.size * piece.shape[1],
            bytes_accessed=8 * piece.size,
            transcendentals=0,
        ),
        name="transform",
    )(piece, table, *held, *after)


def bias_base(count, lanes):
    if lanes % LANES:
        return 0
    first = (lax.axis_index("lag") * count + lax.axis_index("ctx")) * lanes
    return pl.multiple_of(first, LANES)


def inverse(y, back):
    upper = y.astype(jnp.bfloat16)
    lower = (y - upper.astype(jnp.float32)).astype(jnp.bfloat16)
    return dot(back[...], jnp.concatenate([upper, upper, lower], 0)).astype(jnp.bfloat16)


def products(at, shape, bias, sums, total, ready, wanted, closes):
    count, length, both = shape
    rows, lanes = length // 2, both // 2
    width = min(lanes, LANES)
    base = bias_base(count, lanes)
    meets = [[i for i in range(r + 1) if wanted(i, r - i)] for r in range(count)]
    values = sorted({i for r in range(count) for i in meets[r]})
    taps = sorted({r - i for r in range(count) for i in meets[r]})

    def tile(t, sign):
        re = pl.ds(pl.multiple_of(t * 8, 8), 8)
        im = pl.ds(pl.multiple_of(rows + t * 8, 8), 8)
        for first in range(0, lanes, width):
            val = slice(first, first + width)
            tap = slice(lanes + first, lanes + first + width)
            val_re = {i: at(i)[re, val] for i in values}
            val_im = {i: at(i)[im, val] for i in values}
            tap_re = {j: at(j)[re, tap] for j in taps}
            tap_im = {j: at(j)[im, tap] for j in taps}
            if 0 in taps:
                tap_re[0] = tap_re[0] + bias[:, pl.ds(base + first, width)]
            last_re = last_im = None
            for r in range(count):
                sum_re = sum_im = None
                if r in ready:
                    sum_re, sum_im = sums[r, re, val], sums[r, im, val]
                for i in meets[r]:
                    a, b, c, d = val_re[i], val_im[i], tap_re[r - i], tap_im[r - i]
                    new_re, new_im = a * c - b * d, a * d + b * c
                    sum_re = new_re if sum_re is None else sum_re + new_re
                    sum_im = new_im if sum_im is None else sum_im + new_im
                if closes(r):
                    total[r, re, val] = sum_re if r == 0 else sum_re - sign * last_im
                    total[r, im, val] = sum_im if r == 0 else sum_im + sign * last_re
                if sums is not None and meets[r] and r not in ready:
                    sums[r, re, val] = sum_re
                    sums[r, im, val] = sum_im
                last_re, last_im = sum_re, sum_im

    half = rows // 16
    unroll = half if count <= 4 else 1
    pl.loop(0, half, unroll=unroll)(lambda t: tile(t, 1.0))
    pl.loop(half, 2 * half, unroll=unroll)(lambda t: tile(t, -1.0))


def early_kernel(count, last, bias, back, spectra, sums, early, total):
    missing = came(OUT, count, lax.axis_index("ctx"), last)
    for m in range(count):

        @pl.when(missing == m)
        def _(m=m):
            products(
                lambda i: spectra.at[i], spectra.shape, bias, sums, total, (), lambda i, j: m not in (i, j), lambda r: r < m
            )
            for r in range(m):
                early[r] = inverse(total[r], back)


def late_kernel(count, last, piece, bias, forward, back, sums, early, spectra, *refs):
    outs, total, result, fresh = refs[:count], *refs[count:]
    me = lax.axis_index("ctx")
    missing = came(OUT, count, me, last)
    x = piece[...]
    fresh[0] = dot(forward[...], jnp.concatenate([x, x], 0))
    for m in range(count):

        @pl.when(missing == m)
        def _(m=m):
            ready = [r for r in range(count) if any(m not in (i, r - i) for i in range(r + 1))]
            products(
                lambda i: fresh.at[0] if i == m else spectra.at[i], spectra.shape, bias, sums, total, ready, lambda i, j: m in (i, j), lambda r: r >= m
            )
            for r in range(count):
                result[r] = early[r] if r < m else inverse(total[r], back)

    for place, step in enumerate([0] + steps(BACK, count)):
        outs[place][...] = result[to(BACK, count, me, step)]


def whole_kernel(count, last, piece, bias, forward, back, held, *refs):
    outs, total, result, spectra = refs[:count], *refs[count:]
    spectra[...] = held[...]
    me = lax.axis_index("ctx")
    transform_into(OUT, last, piece, forward, spectra)
    products(lambda i: spectra.at[i], spectra.shape, bias, None, total, (), lambda i, j: True, lambda r: True)
    for r in range(count):
        result[r] = inverse(total[r], back)
    for place, step in enumerate([0] + steps(BACK, count)):
        outs[place][...] = result[to(BACK, count, me, step)]


def convolve(spectra, last, piece, bias, forward, back):
    count, length, both = spectra.shape
    rows, lanes = length // 2, both // 2
    totals = jax.ShapeDtypeStruct((count, length, lanes), jnp.float32)
    results = jax.ShapeDtypeStruct((count, rows, lanes), jnp.bfloat16)
    held = []
    if count <= 4:
        held = pl.pallas_call(
            functools.partial(early_kernel, count, last),
            out_shape=[totals, results],
            in_specs=[VMEM] * 3,
            out_specs=[VMEM] * 2,
            scratch_shapes=[pltpu.VMEM(totals.shape, totals.dtype)],
            compiler_params=pltpu.CompilerParams(vmem_limit_bytes=4 * MIB),
            cost_estimate=pl.CostEstimate(
                flops=3 * 2 * back.size * lanes, bytes_accessed=4 * spectra.size, transcendentals=0
            ),
            name="early_products",
        )(bias, back, spectra)
    return pl.pallas_call(
        functools.partial(late_kernel if held else whole_kernel, count, last),
        out_shape=[jax.ShapeDtypeStruct((rows, lanes), jnp.bfloat16)] * count,
        in_specs=[VMEM] * (5 + len(held)),
        out_specs=[VMEM] * count,
        scratch_shapes=[
            pltpu.VMEM(totals.shape, totals.dtype),
            pltpu.VMEM(results.shape, results.dtype),
            pltpu.VMEM((1 if held else count, length, both), jnp.float32),
        ],
        compiler_params=pltpu.CompilerParams(vmem_limit_bytes=8 * MIB),
        name="convolve",
    )(piece, bias, forward, back, *held, spectra)


def gated(gate, cols, piece):
    return (gate[:, cols].astype(jnp.float32) * piece.astype(jnp.float32)).astype(jnp.bfloat16)


def first_block_kernel(count, lanes, *refs):
    pieces = refs[: count - 1]
    bias, forward, back, gate, out, token, spectrum, total, mixed, sem = refs[count - 1 :]
    rows = out.shape[0]
    lag = lax.axis_index("lag")
    token[...] = jnp.zeros_like(token)

    @pl.when(lax.axis_index("ctx") == 0)
    def _():
        for step, piece in zip(steps(OUT, count), pieces):
            owner = step
            cols = slice(owner * lanes, (owner + 1) * lanes)
            x = piece[...]
            spectrum[...] = dot(forward[...], jnp.concatenate([x, x], 0))
            start = pl.multiple_of((lag * count + owner) * lanes, LANES)
            a, b = spectrum[:rows, :lanes], spectrum[rows:, :lanes]
            c = spectrum[:rows, lanes:] + bias[:, pl.ds(start, lanes)]
            d = spectrum[rows:, lanes:]
            total[:rows] = a * c - b * d
            total[rows:] = a * d + b * c
            mixed[:, cols] = gated(gate, cols, inverse(total[...], back))
        copy = pltpu.make_async_copy(mixed.at[:, lanes:], out.at[:, lanes:], sem)
        copy.start()
        copy.wait()


def first_block(pieces, bias, forward, back, gate):
    count = len(pieces) + 1
    lanes = pieces[0].shape[1] // 2
    length = forward.shape[0]
    return pl.pallas_call(
        functools.partial(first_block_kernel, count, lanes),
        out_shape=[
            jax.ShapeDtypeStruct(gate.shape, jnp.bfloat16),
            jax.ShapeDtypeStruct((8, LANES), jnp.float32),
        ],
        in_specs=[VMEM] * (count + 3),
        out_specs=[pl.BlockSpec(memory_space=pltpu.HBM), VMEM],
        scratch_shapes=[
            pltpu.VMEM((length, 2 * lanes), jnp.float32),
            pltpu.VMEM((length, lanes), jnp.float32),
            pltpu.VMEM(gate.shape, jnp.bfloat16),
            pltpu.SemaphoreType.DMA,
        ],
        compiler_params=pltpu.CompilerParams(vmem_limit_bytes=4 * MIB),
        cost_estimate=pl.CostEstimate(
            flops=2 * (count - 1) * forward.size * 2 * lanes, bytes_accessed=0, transcendentals=0
        ),
        name="first_block",
    )(*pieces, bias, forward, back, gate)


def put_kernel(places, count, *refs):
    pieces, gate, out, mixed, sems = refs[: len(places)], refs[-5], refs[-3], refs[-2], refs[-1]
    lanes = pieces[0].shape[1]
    me = lax.axis_index("ctx")
    order = [0] + steps(BACK, count)

    def put(todo):
        copies = []
        for k in todo:
            owner = came(BACK, count, me, order[places[k]])
            cols = pl.ds(pl.multiple_of(owner * lanes, LANES), lanes)
            mixed[k] = gated(gate, cols, pieces[k][...])
            copies.append(pltpu.make_async_copy(mixed.at[k], out.at[:, cols], sems.at[k]))
            copies[-1].start()
        for copy in copies:
            copy.wait()

    mine = [k for k, place in enumerate(places) if place == 0]
    if mine:
        put(mine)

    @pl.when(me != 0)
    def _():
        put([k for k in range(len(places)) if k not in mine])


def put(places, pieces, gate, out):
    count = gate.shape[1] // pieces[0].shape[1]
    hbm = pl.BlockSpec(memory_space=pltpu.HBM)
    return pl.pallas_call(
        functools.partial(put_kernel, places, count),
        out_shape=jax.ShapeDtypeStruct(gate.shape, jnp.bfloat16),
        in_specs=[VMEM] * (len(pieces) + 1) + [hbm],
        out_specs=hbm,
        scratch_shapes=[
            pltpu.VMEM((len(places),) + pieces[0].shape, jnp.bfloat16),
            pltpu.SemaphoreType.DMA((len(places),)),
        ],
        input_output_aliases={len(pieces) + 1: 0},
        compiler_params=pltpu.CompilerParams(vmem_limit_bytes=MIB),
        name="put",
    )(*pieces, gate, out)


def apply_gate(returned, gate):
    me = lax.axis_index("ctx")
    ordered = jnp.roll(jnp.stack(returned)[::-1], me + 1, 0)
    whole = jnp.transpose(ordered, (1, 0, 2)).reshape(gate.shape)
    return (gate.astype(jnp.float32) * whole.astype(jnp.float32)).astype(jnp.bfloat16)


def move(plan, count, step, piece):
    return lax.ppermute(piece, "ctx", pairs(plan, count, step))


def body(values, gate, bias, filter_taps):
    rows, share = gate.shape
    count = lax.axis_size("ctx")
    lanes = share // count
    forward, back = (jnp.asarray(table) for table in dft_tables(rows))
    own_bias = bias.reshape(1, -1)
    if lanes % LANES:
        start = (lax.axis_index("lag") * count + lax.axis_index("ctx")) * lanes
        own_bias = lax.dynamic_slice_in_dim(own_bias, start, lanes, 1)
    own, pieces = take(values, filter_taps, count, lanes)
    out_steps, back_steps = steps(OUT, count), steps(BACK, count)
    arrived = [move(OUT, count, step, piece) for step, piece in zip(out_steps, pieces)]
    spectra = transform(None, 0, own, forward, count)
    after = []
    if lanes % LANES == 0:
        out, *after = first_block(pieces, own_bias, forward, back, gate)
    for step, piece in zip(out_steps[:-1], arrived):
        spectra = transform(spectra, step, piece, forward, count, after)
        after = []
    done = convolve(spectra, out_steps[-1], arrived[-1], own_bias, forward, back)
    returned = [move(BACK, count, step, piece) for step, piece in zip(back_steps, done[1:])]
    if lanes % LANES:
        return apply_gate([done[0]] + returned, gate)
    out = put((0,), done[:1], gate, out)
    return put(tuple(range(1, count)), returned, gate, out)


def solution(mesh):
    return jax.shard_map(
        body,
        mesh=mesh,
        in_specs=(P("ctx", "chan"), P("ctx", ("chan", "lag")), P("chan"), P("ctx", "chan")),
        out_specs=P("ctx", ("chan", "lag")),
        check_vma=False,
    )
```

```python
import functools

import jax
import jax.numpy as jnp
import ml_dtypes
import numpy as np
from jax import lax
from jax.experimental import pallas as pl
from jax.experimental.pallas import tpu as pltpu
from jax.sharding import PartitionSpec as P

LANES = 128
MIB = 1 << 20
VMEM = pl.BlockSpec(memory_space=pltpu.VMEM)
OUT = ("swap", 3, 1, 2)
BACK = ("swap", 2, 3, 1)


def split(table):
    upper = table.astype(ml_dtypes.bfloat16)
    lower = (table - upper.astype(np.float64)).astype(ml_dtypes.bfloat16)
    return upper, lower


def dft_tables(rows):
    length = 2 * rows
    frequency = np.concatenate([np.arange(0, rows, 2), np.arange(1, rows, 2)])
    odd = 2 * frequency[:, None] + 1
    angle = 2.0 * np.pi * (odd * np.arange(rows)[None, :] % (2 * length)) / (2 * length)
    forward = np.concatenate([np.cos(angle), -np.sin(angle)], 0)
    back = np.concatenate([np.cos(angle.T), -np.sin(angle.T)], 1) / rows
    upper, lower = split(back)
    return np.concatenate(split(forward), 1), np.concatenate([upper, lower, upper], 1)


def steps(plan, count):
    return list(plan[1:]) if count == 4 else list(range(1, count))


def swaps(plan, count):
    return plan[0] == "swap" and count & (count - 1) == 0


def to(plan, count, me, step):
    return me ^ step if swaps(plan, count) else lax.rem(me + step, count)


def came(plan, count, me, step):
    return me ^ step if swaps(plan, count) else lax.rem(me - step + count, count)


def pairs(plan, count, step):
    if swaps(plan, count):
        return [(i, i ^ step) for i in range(count)]
    return [(i, (i + step) % count) for i in range(count)]


def dot(a, b):
    return jnp.dot(a, b, preferred_element_type=jnp.float32)


def take(values, taps, count, lanes):
    me = lax.axis_index("ctx")
    first = lax.axis_index("lag") * (count * lanes)
    later = lax.optimization_barrier((values, taps))

    def piece(step, arrays):
        start = first + to(OUT, count, me, step) * lanes
        return jnp.concatenate(
            [lax.dynamic_slice_in_dim(array, start, lanes, 1) for array in arrays], 1
        )

    order = steps(OUT, count)
    pieces = {step: piece(step, (values, taps) if step == order[0] else later) for step in order}
    return piece(0, later), [pieces[step] for step in order]


def transform_into(plan, step, piece, table, spectra):
    count = spectra.shape[0]
    x = piece[...]
    owner = came(plan, count, lax.axis_index("ctx"), step)
    spectra[owner] = dot(table[...], jnp.concatenate([x, x], 0))


def transform_kernel(step, *refs):
    piece, table, spectra = refs[0], refs[1], refs[-1]
    if step:
        spectra[...] = refs[2][...]
    transform_into(OUT, step, piece, table, spectra)


def transform(spectra, step, piece, table, count, after=()):
    shape = jax.ShapeDtypeStruct((count, table.shape[0], piece.shape[1]), jnp.float32)
    held = [] if spectra is None else [spectra]
    return pl.pallas_call(
        functools.partial(transform_kernel, step),
        out_shape=shape,
        in_specs=[VMEM] * (2 + len(held) + len(after)),
        out_specs=VMEM,
        input_output_aliases={2: 0} if held else {},
        compiler_params=pltpu.CompilerParams(vmem_limit_bytes=2 * MIB),
        cost_estimate=pl.CostEstimate(
            flops=2 * table.size * piece.shape[1],
            bytes_accessed=8 * piece.size,
            transcendentals=0,
        ),
        name="transform",
    )(piece, table, *held, *after)


def bias_base(count, lanes):
    if lanes % LANES:
        return 0
    first = (lax.axis_index("lag") * count + lax.axis_index("ctx")) * lanes
    return pl.multiple_of(first, LANES)


def inverse(y, back):
    upper = y.astype(jnp.bfloat16)
    lower = (y - upper.astype(jnp.float32)).astype(jnp.bfloat16)
    return dot(back[...], jnp.concatenate([upper, upper, lower], 0)).astype(jnp.bfloat16)


def products(at, shape, bias, sums, total, ready, wanted, closes):
    count, length, both = shape
    rows, lanes = length // 2, both // 2
    width = min(lanes, LANES)
    base = bias_base(count, lanes)
    meets = [[i for i in range(r + 1) if wanted(i, r - i)] for r in range(count)]
    values = sorted({i for r in range(count) for i in meets[r]})
    taps = sorted({r - i for r in range(count) for i in meets[r]})

    def tile(t, sign):
        re = pl.ds(pl.multiple_of(t * 8, 8), 8)
        im = pl.ds(pl.multiple_of(rows + t * 8, 8), 8)
        for first in range(0, lanes, width):
            val = slice(first, first + width)
            tap = slice(lanes + first, lanes + first + width)
            val_re = {i: at(i)[re, val] for i in values}
            val_im = {i: at(i)[im, val] for i in values}
            tap_re = {j: at(j)[re, tap] for j in taps}
            tap_im = {j: at(j)[im, tap] for j in taps}
            if 0 in taps:
                tap_re[0] = tap_re[0] + bias[:, pl.ds(base + first, width)]
            last_re = last_im = None
            for r in range(count):
                sum_re = sum_im = None
                if r in ready:
                    sum_re, sum_im = sums[r, re, val], sums[r, im, val]
                for i in meets[r]:
                    a, b, c, d = val_re[i], val_im[i], tap_re[r - i], tap_im[r - i]
                    new_re, new_im = a * c - b * d, a * d + b * c
                    sum_re = new_re if sum_re is None else sum_re + new_re
                    sum_im = new_im if sum_im is None else sum_im + new_im
                if closes(r):
                    total[r, re, val] = sum_re if r == 0 else sum_re - sign * last_im
                    total[r, im, val] = sum_im if r == 0 else sum_im + sign * last_re
                if sums is not None and meets[r] and r not in ready:
                    sums[r, re, val] = sum_re
                    sums[r, im, val] = sum_im
                last_re, last_im = sum_re, sum_im

    half = rows // 16
    unroll = half if count <= 4 else 1
    pl.loop(0, half, unroll=unroll)(lambda t: tile(t, 1.0))
    pl.loop(half, 2 * half, unroll=unroll)(lambda t: tile(t, -1.0))


def early_kernel(count, last, bias, back, spectra, sums, early, total):
    missing = came(OUT, count, lax.axis_index("ctx"), last)
    for m in range(count):

        @pl.when(missing == m)
        def _(m=m):
            products(
                lambda i: spectra.at[i], spectra.shape, bias, sums, total, (), lambda i, j: m not in (i, j), lambda r: r < m
            )
            for r in range(m):
                early[r] = inverse(total[r], back)


def late_kernel(count, last, piece, bias, forward, back, sums, early, spectra, *refs):
    outs, total, result, fresh = refs[:count], *refs[count:]
    me = lax.axis_index("ctx")
    missing = came(OUT, count, me, last)
    x = piece[...]
    fresh[0] = dot(forward[...], jnp.concatenate([x, x], 0))
    for m in range(count):

        @pl.when(missing == m)
        def _(m=m):
            ready = [r for r in range(count) if any(m not in (i, r - i) for i in range(r + 1))]
            products(
                lambda i: fresh.at[0] if i == m else spectra.at[i], spectra.shape, bias, sums, total, ready, lambda i, j: m in (i, j), lambda r: r >= m
            )
            for r in range(count):
                result[r] = early[r] if r < m else inverse(total[r], back)

    for place, step in enumerate([0] + steps(BACK, count)):
        outs[place][...] = result[to(BACK, count, me, step)]


def whole_kernel(count, last, piece, bias, forward, back, held, *refs):
    outs, total, result, spectra = refs[:count], *refs[count:]
    spectra[...] = held[...]
    me = lax.axis_index("ctx")
    transform_into(OUT, last, piece, forward, spectra)
    products(lambda i: spectra.at[i], spectra.shape, bias, None, total, (), lambda i, j: True, lambda r: True)
    for r in range(count):
        result[r] = inverse(total[r], back)
    for place, step in enumerate([0] + steps(BACK, count)):
        outs[place][...] = result[to(BACK, count, me, step)]


def convolve(spectra, last, piece, bias, forward, back):
    count, length, both = spectra.shape
    rows, lanes = length // 2, both // 2
    totals = jax.ShapeDtypeStruct((count, length, lanes), jnp.float32)
    results = jax.ShapeDtypeStruct((count, rows, lanes), jnp.bfloat16)
    held = []
    if count <= 4:
        held = pl.pallas_call(
            functools.partial(early_kernel, count, last),
            out_shape=[totals, results],
            in_specs=[VMEM] * 3,
            out_specs=[VMEM] * 2,
            scratch_shapes=[pltpu.VMEM(totals.shape, totals.dtype)],
            compiler_params=pltpu.CompilerParams(vmem_limit_bytes=4 * MIB),
            cost_estimate=pl.CostEstimate(
                flops=3 * 2 * back.size * lanes, bytes_accessed=4 * spectra.size, transcendentals=0
            ),
            name="early_products",
        )(bias, back, spectra)
    return pl.pallas_call(
        functools.partial(late_kernel if held else whole_kernel, count, last),
        out_shape=[jax.ShapeDtypeStruct((rows, lanes), jnp.bfloat16)] * count,
        in_specs=[VMEM] * (5 + len(held)),
        out_specs=[VMEM] * count,
        scratch_shapes=[
            pltpu.VMEM(totals.shape, totals.dtype),
            pltpu.VMEM(results.shape, results.dtype),
            pltpu.VMEM((1 if held else count, length, both), jnp.float32),
        ],
        compiler_params=pltpu.CompilerParams(vmem_limit_bytes=8 * MIB),
        name="convolve",
    )(piece, bias, forward, back, *held, spectra)


def gated(gate, cols, piece):
    return (gate[:, cols].astype(jnp.float32) * piece.astype(jnp.float32)).astype(jnp.bfloat16)


def first_block_kernel(count, lanes, *refs):
    pieces = refs[: count - 1]
    bias, forward, back, gate, out, token, spectrum, total, mixed, sem = refs[count - 1 :]
    rows = out.shape[0]
    lag = lax.axis_index("lag")
    token[...] = jnp.zeros_like(token)

    @pl.when(lax.axis_index("ctx") == 0)
    def _():
        for step, piece in zip(steps(OUT, count), pieces):
            owner = step
            cols = slice(owner * lanes, (owner + 1) * lanes)
            x = piece[...]
            spectrum[...] = dot(forward[...], jnp.concatenate([x, x], 0))
            start = pl.multiple_of((lag * count + owner) * lanes, LANES)
            a, b = spectrum[:rows, :lanes], spectrum[rows:, :lanes]
            c = spectrum[:rows, lanes:] + bias[:, pl.ds(start, lanes)]
            d = spectrum[rows:, lanes:]
            total[:rows] = a * c - b * d
            total[rows:] = a * d + b * c
            mixed[:, cols] = gated(gate, cols, inverse(total[...], back))
        copy = pltpu.make_async_copy(mixed.at[:, lanes:], out.at[:, lanes:], sem)
        copy.start()
        copy.wait()


def first_block(pieces, bias, forward, back, gate):
    count = len(pieces) + 1
    lanes = pieces[0].shape[1] // 2
    length = forward.shape[0]
    return pl.pallas_call(
        functools.partial(first_block_kernel, count, lanes),
        out_shape=[
            jax.ShapeDtypeStruct(gate.shape, jnp.bfloat16),
            jax.ShapeDtypeStruct((8, LANES), jnp.float32),
        ],
        in_specs=[VMEM] * (count + 3),
        out_specs=[pl.BlockSpec(memory_space=pltpu.HBM), VMEM],
        scratch_shapes=[
            pltpu.VMEM((length, 2 * lanes), jnp.float32),
            pltpu.VMEM((length, lanes), jnp.float32),
            pltpu.VMEM(gate.shape, jnp.bfloat16),
            pltpu.SemaphoreType.DMA,
        ],
        compiler_params=pltpu.CompilerParams(vmem_limit_bytes=4 * MIB),
        cost_estimate=pl.CostEstimate(
            flops=2 * (count - 1) * forward.size * 2 * lanes, bytes_accessed=0, transcendentals=0
        ),
        name="first_block",
    )(*pieces, bias, forward, back, gate)


def put_kernel(places, count, *refs):
    pieces, gate, out, mixed, sems = refs[: len(places)], refs[-5], refs[-3], refs[-2], refs[-1]
    lanes = pieces[0].shape[1]
    me = lax.axis_index("ctx")
    order = [0] + steps(BACK, count)

    def put(todo):
        copies = []
        for k in todo:
            owner = came(BACK, count, me, order[places[k]])
            cols = pl.ds(pl.multiple_of(owner * lanes, LANES), lanes)
            mixed[k] = gated(gate, cols, pieces[k][...])
            copies.append(pltpu.make_async_copy(mixed.at[k], out.at[:, cols], sems.at[k]))
            copies[-1].start()
        for copy in copies:
            copy.wait()

    mine = [k for k, place in enumerate(places) if place == 0]
    if mine:
        put(mine)

    @pl.when(me != 0)
    def _():
        put([k for k in range(len(places)) if k not in mine])


def put(places, pieces, gate, out):
    count = gate.shape[1] // pieces[0].shape[1]
    hbm = pl.BlockSpec(memory_space=pltpu.HBM)
    return pl.pallas_call(
        functools.partial(put_kernel, places, count),
        out_shape=jax.ShapeDtypeStruct(gate.shape, jnp.bfloat16),
        in_specs=[VMEM] * (len(pieces) + 1) + [hbm],
        out_specs=hbm,
        scratch_shapes=[
            pltpu.VMEM((len(places),) + pieces[0].shape, jnp.bfloat16),
            pltpu.SemaphoreType.DMA((len(places),)),
        ],
        input_output_aliases={len(pieces) + 1: 0},
        compiler_params=pltpu.CompilerParams(vmem_limit_bytes=MIB),
        name="put",
    )(*pieces, gate, out)


def apply_gate(returned, gate):
    me = lax.axis_index("ctx")
    ordered = jnp.roll(jnp.stack(returned)[::-1], me + 1, 0)
    whole = jnp.transpose(ordered, (1, 0, 2)).reshape(gate.shape)
    return (gate.astype(jnp.float32) * whole.astype(jnp.float32)).astype(jnp.bfloat16)


def move(plan, count, step, piece):
    return lax.ppermute(piece, "ctx", pairs(plan, count, step))


def body(values, gate, bias, filter_taps):
    rows, share = gate.shape
    count = lax.axis_size("ctx")
    lanes = share // count
    forward, back = (jnp.asarray(table) for table in dft_tables(rows))
    own_bias = bias.reshape(1, -1)
    if lanes % LANES:
        start = (lax.axis_index("lag") * count + lax.axis_index("ctx")) * lanes
        own_bias = lax.dynamic_slice_in_dim(own_bias, start, lanes, 1)
    own, pieces = take(values, filter_taps, count, lanes)
    out_steps, back_steps = steps(OUT, count), steps(BACK, count)
    arrived = [move(OUT, count, step, piece) for step, piece in zip(out_steps, pieces)]
    spectra = transform(None, 0, own, forward, count)
    after = []
    if lanes % LANES == 0:
        out, *after = first_block(pieces, own_bias, forward, back, gate)
    for step, piece in zip(out_steps[:-1], arrived):
        spectra = transform(spectra, step, piece, forward, count, after)
        after = []
    done = convolve(spectra, out_steps[-1], arrived[-1], own_bias, forward, back)
    returned = [move(BACK, count, step, piece) for step, piece in zip(back_steps, done[1:])]
    if lanes % LANES:
        return apply_gate([done[0]] + returned, gate)
    out = put((0,), done[:1], gate, out)
    return put(tuple(range(1, count)), returned, gate, out)


def solution(mesh):
    return jax.shard_map(
        body,
        mesh=mesh,
        in_specs=(P("ctx", "chan"), P("ctx", ("chan", "lag")), P("chan"), P("ctx", "chan")),
        out_specs=P("ctx", ("chan", "lag")),
        check_vma=False,
    )
```
